256 devices in a mesh: row: 8 (over z_lo, x), col: 32 (over y, z_hi, core).
Axes of the slice: x: 4, y: 4, z: 8 (z_hi: 4, z_lo: 2; z = z_hi * 2 + z_lo), core: 2. Of those that a mesh axis runs over, the one named last changes fastest.
Arguments:
- tokens: bfloat16 [512, 8192], P('col', 'row'), may hold values from -6 to 6
- grad_output: bfloat16 [512, 8192], P('col', 'row'), may hold values from -1.5 to 1.5
- gate_weight: bfloat16 [8192, 28672], P('row', 'col'), may hold values from -0.0625 to 0.0625
- up_weight: bfloat16 [8192, 28672], P('row', 'col'), may hold values from -0.0625 to 0.0625
- down_weight: bfloat16 [28672, 8192], P('col', 'row'), may hold values from -0.03125 to 0.03125
- segment_ids: int32 [512], replicated, may hold values from 0 to 63, never falling along the last dimension, each value on 1 to 16 neighbouring positions
Outputs:
- grad_tokens: bfloat16 [512, 8192], P('col', 'row')
- grad_gate: bfloat16 [8192, 28672], P('row', 'col')
- grad_up: bfloat16 [8192, 28672], P('row', 'col')
- grad_down: bfloat16 [28672, 8192], P('col', 'row')
The draws below stay inside these ranges and needn't reach their ends.
Inputs may be any that keep to these rules, and one draw needn't show every extreme that they name: `segment_ids`: segment ids never fall along the tokens; each of the 64 passages holds 1 to 16 tokens, one exactly 16.
All inputs are finite; a program needn't handle non-finite values.
Results may differ from the reference program's by a relative error of at most 0.033.
Values may be sent and summed in bfloat16 or wider, within the bound.
A program may use at most 64 MiB of HBM per device.

```python
import math
import jax
import jax.numpy as jnp
import numpy as np
from jax import lax

D = 8192
FF = 28672
TOKENS = 512
MOST = 16
SEGS = 64
N_ROW = 8


def block_levels(key, dims, shards, least, top_value):
    def one(dim, blocks):
        heights = jax.random.uniform(jax.random.fold_in(jax.random.fold_in(key, 6), dim), (blocks,), jnp.float32, least / len(shards), top_value / len(shards))
        return jnp.repeat(jnp.exp(heights), dims[dim] // blocks).reshape((-1,) + (1,) * (len(dims) - dim - 1))

    gain = one(*shards[0])
    for cut in shards[1:]:
        gain = gain * one(*cut)
    return gain


def split_up(count, total, limit, slope):
    weights = [(1 << 20) // math.isqrt(rank ** slope) + 1 for rank in range(2, count + 1)]
    surplus, given = total - limit - (count - 1), [1] * (count - 1)
    while surplus > 0:
        free = [i for i in range(count - 1) if given[i] < limit]
        mass, budget = sum([weights[i] for i in free]), surplus
        for i in free:
            more = min(limit - given[i], max(1, budget * weights[i] // mass), surplus)
            given[i] = given[i] + more
            surplus = surplus - more
    return np.array([limit] + given)


def ragged(stream_key, number_of, total, reach, skew):
    if number_of == 2:
        one = jax.random.randint(stream_key, (), max(1, total - reach), min(reach, total - 1) + 1)
        return jnp.stack([one, total - one])
    tallies = jnp.asarray(split_up(number_of, total, reach, skew), jnp.int32)
    couples = (number_of - 1) // 2
    donor, taker = tallies[1:1 + 2 * couples:2], tallies[2:2 + 2 * couples:2]
    margin = jnp.minimum(donor - 1, reach - taker)
    passed = jax.random.randint(jax.random.fold_in(stream_key, 1), (couples,), 0, 1 << 20) % (margin + 1)
    tallies = tallies.at[1:1 + 2 * couples:2].set(donor - passed).at[2:2 + 2 * couples:2].set(taker + passed)
    return tallies[jax.random.permutation(jax.random.fold_in(stream_key, 2), number_of)]


def bell_draw(stream_key, dims, scale, limit, cuts=(), kind=jnp.bfloat16):
    values = jax.random.normal(stream_key, dims, jnp.float32) * scale
    if len(cuts) > 0:
        values = block_levels(stream_key, dims, cuts, -0.22, 0.18) * values
    return jnp.clip(values, min=-limit, max=limit).astype(kind)


def setup_inputs(seed: int = 0) -> dict:
    key_list = jax.random.split(jax.random.key(seed), 7)
    tokens = bell_draw(key_list[0], (TOKENS, D), 1.0, 6.0, ((0, 32), (1, 8)))
    grad_output = bell_draw(key_list[1], (TOKENS, D), 0.25, 1.5, ((0, 32), (1, 8)))
    gate_weight = bell_draw(key_list[2], (D, FF), D ** -0.5, 0.0625, ((0, 8), (1, 32)))
    up_weight = bell_draw(key_list[3], (D, FF), D ** -0.5, 0.0625, ((0, 8), (1, 32)))
    down_weight = bell_draw(key_list[4], (FF, D), FF ** -0.5, 0.03125, ((0, 32), (1, 8)))
    segment_ids = jnp.searchsorted(jnp.cumsum(ragged(key_list[5], SEGS, TOKENS, MOST, 0)), jnp.arange(TOKENS), side="right").astype(jnp.int32)
    return dict(tokens=tokens, grad_output=grad_output, gate_weight=gate_weight, up_weight=up_weight, down_weight=down_weight, segment_ids=segment_ids)


def rounded(value):
    return lax.optimization_barrier(value.astype(jnp.bfloat16)).astype(jnp.float32)


def reference(tokens, grad_output, gate_weight, up_weight, down_weight, segment_ids):
    width = D // N_ROW
    same = segment_ids[:, None] == segment_ids[None, :]
    counts = jnp.sum(same.astype(jnp.float32), axis=1)
    token_weight = (TOKENS / SEGS) / counts
    weighted = (grad_output.astype(jnp.float32) * token_weight[:, None]).astype(jnp.bfloat16)
    gate = jnp.zeros((TOKENS, FF), jnp.float32)
    up = jnp.zeros((TOKENS, FF), jnp.float32)
    d_hidden = jnp.zeros((TOKENS, FF), jnp.float32)
    for block in range(N_ROW):
        low = block * width
        high = low + width
        piece = tokens[:, low:high]
        gate = gate + rounded(jnp.dot(piece, gate_weight[low:high], preferred_element_type=jnp.float32))
        up = up + rounded(jnp.dot(piece, up_weight[low:high], preferred_element_type=jnp.float32))
        d_hidden = d_hidden + rounded(jnp.dot(weighted[:, low:high], down_weight[:, low:high].T, preferred_element_type=jnp.float32))
    sig = jax.nn.sigmoid(gate)
    hidden = (gate * sig * up).astype(jnp.bfloat16)
    d_gate = (d_hidden * up * sig * (1.0 + gate * (1.0 - sig))).astype(jnp.bfloat16)
    d_up = (d_hidden * gate * sig).astype(jnp.bfloat16)
    grad_down = jnp.dot(hidden.T, weighted, preferred_element_type=jnp.float32).astype(jnp.bfloat16)
    grad_gate = jnp.dot(tokens.T, d_gate, preferred_element_type=jnp.float32).astype(jnp.bfloat16)
    grad_up = jnp.dot(tokens.T, d_up, preferred_element_type=jnp.float32).astype(jnp.bfloat16)
    grad_tokens = jnp.dot(d_gate, gate_weight.T, preferred_element_type=jnp.float32) + jnp.dot(d_up, up_weight.T, preferred_element_type=jnp.float32)
    return grad_tokens.astype(jnp.bfloat16), grad_gate, grad_up, grad_down
```

```python
import functools

import jax
import jax.numpy as jnp
from jax import lax
from jax.experimental import pallas as pl
from jax.experimental.pallas import tpu as pltpu
from jax.sharding import PartitionSpec as P

MESH = pl.DeviceIdType.MESH
BF = jnp.bfloat16
F32 = jnp.float32
TOKENS = 512
SEGS = 64
G = 16
ORDER = (0, 1, 3, 2)
KINDS = "xxxx"


def nn(a, b):
    return jnp.dot(a, b, preferred_element_type=F32)


def nt(a, b):
    return lax.dot_general(a, b, (((1,), (1,)), ((), ())), preferred_element_type=F32)


def kernel(
    tokens, grad, ids, gate_w, up_w, down_w,
    o_tok, o_gate, o_up, o_down,
    tw, gst, gw, uw, dw, part, relp, relm, land, zs, zr, zbig, hid, gt, sib, ysend, yland,
    zsend, zland, own, tok_t, hid_t, w_st, og, ou, od,
    ssem, loc, a_recv, p_recv, l_recv, z_recv, h_recv, h2_recv, s_recv, y_recv, zh_recv,
):
    f = gw.shape[1]
    d = gw.shape[0]
    cut = (3 * f // 256 + 1) * 128
    r, c = lax.axis_index("row"), lax.axis_index("col")
    x, zl = r % 4, r // 4
    core, zh, y = c % 2, (c // 2) % 4, c // 8
    xp, xm, x2 = (x + 1) % 4, (x + 3) % 4, (x + 2) % 4

    def at(x=x, zl=zl, y=y, zh=zh, core=core):
        return {"row": zl * 4 + x, "col": (y * 4 + zh) * 2 + core}

    dev_xp, dev_xm, dev_z, dev_core = at(x=xp), at(x=xm), at(zl=1 - zl), at(core=1 - core)
    dev_zh = [at(zh=(zh + k) % 4) for k in (1, 2, 3)]
    dev_y = [at(y=(y + k) % 4) for k in (1, 2, 3)]
    partners = [dev_xp, dev_xm, dev_z, dev_core] + dev_zh + dev_y

    barrier = pltpu.get_barrier_semaphore()
    for p in partners:
        pl.semaphore_signal(barrier, inc=1, device_id=p, device_id_type=MESH)

    first = [
        pltpu.make_async_copy(tokens, tw.at[y, core, zh, 0], loc.at[0]),
        pltpu.make_async_copy(grad, gst, loc.at[1]),
    ]
    weights = [
        pltpu.make_async_copy(gate_w, gw, loc.at[2]),
        pltpu.make_async_copy(up_w, uw, loc.at[3]),
        pltpu.make_async_copy(down_w, dw, loc.at[4]),
    ]
    for cp in first + weights:
        cp.start()

    idr = jnp.broadcast_to(ids[...].astype(F32), (G, TOKENS))
    lane = lax.broadcasted_iota(jnp.int32, (G, TOKENS), 1)
    row = lax.broadcasted_iota(jnp.int32, (G, TOKENS), 0)
    mine = jnp.sum(jnp.where(lane == c * G + row, idr, 0.0), axis=1, keepdims=True)
    count = jnp.sum(jnp.where(idr == mine, 1.0, 0.0), axis=1, keepdims=True)
    weight = (TOKENS / SEGS) / count
    for cp in first:
        cp.wait()
    tw[y, core, zh, 1] = (gst[...].astype(F32) * weight).astype(BF)
    pl.semaphore_wait(barrier, len(partners))

    sent = []

    def push(src, dst, recv, dev):
        cp = pltpu.make_async_remote_copy(
            src_ref=src, dst_ref=dst, send_sem=ssem.at[len(sent)], recv_sem=recv,
            device_id=dev, device_id_type=MESH,
        )
        cp.start()
        sent.append(cp)

    def arrived(ref, recv):
        pltpu.make_async_remote_copy(
            src_ref=ref, dst_ref=ref, send_sem=ssem.at[0], recv_sem=recv,
            device_id=dev_core, device_id_type=MESH,
        ).wait_recv()

    def spread(hh, targets):
        piece = tw.at[y, core, hh]
        for dev in targets:
            push(piece, piece, a_recv.at[y, core, hh], dev)

    def gather_own():
        spread(zh, [dev_zh[0], dev_zh[2], dev_zh[1]])
        spread(zh, [dev_y[0], dev_y[2], dev_y[1], dev_core])
        for k in (1, 3, 2):
            hh = (zh + k) % 4
            arrived(tw.at[y, core, hh], a_recv.at[y, core, hh])
            spread(hh, [dev_y[0], dev_y[2], dev_y[1], dev_core])

    def gather_far(j):
        yy = (y + ORDER[j]) % 4
        for hh in range(4):
            piece = tw.at[yy, core, hh]
            arrived(piece, a_recv.at[yy, core, hh])
            push(piece, piece, a_recv.at[yy, core, hh], dev_core)

    def multiply(j):
        yy = (y + ORDER[j]) % 4
        for hh in range(4):
            arrived(tw.at[yy, 1 - core, hh], a_recv.at[yy, 1 - core, hh])
        t = tw[yy, :, :, 0].reshape(8 * G, d)
        w = tw[yy, :, :, 1].reshape(8 * G, d)
        if j == 0:
            for cp in weights:
                cp.wait()
        part[j, :, :, :, 0:f] = nn(t, gw[...]).astype(BF).reshape(2, 4, G, f)
        part[j, :, :, :, f : 2 * f] = nn(t, uw[...]).astype(BF).reshape(2, 4, G, f)
        part[j, :, :, :, 2 * f : 3 * f] = nt(w, dw[...]).astype(BF).reshape(2, 4, G, f)
        if KINDS[j] == "z":
            push(part.at[j, 1 - zl], zbig.at[j], z_recv.at[j], dev_z)
        else:
            relay(j)
        tok_t[:, j * 8 * G : (j + 1) * 8 * G] = t.T
        w_st[j * 8 * G : (j + 1) * 8 * G, :] = w

    def span(j):
        return pl.ds(zl, 1) if KINDS[j] == "z" else pl.ds(0, 2)

    def slot(j):
        return pl.ds(0, 1) if KINDS[j] == "z" else pl.ds(0, 2)

    def relay(j):
        push(part.at[j, span(j), x2, :, :cut], relp.at[j, slot(j)], p_recv.at[j, 0], dev_xp)
        push(part.at[j, span(j), x2, :, cut:], relm.at[j, slot(j)], p_recv.at[j, 1], dev_xm)

    def pair_first(j):
        if KINDS[j] != "z":
            return
        arrived(zbig.at[j], z_recv.at[j])
        part[j, zl] = (part[j, zl].astype(F32) + zbig[j].astype(F32)).astype(BF)
        relay(j)

    def forward(j):
        s, k = span(j), slot(j)
        arrived(relp.at[j, k], p_recv.at[j, 0])
        part[j, s, xp, :, :cut] = (
            part[j, s, xp, :, :cut].astype(F32) + relp[j, k].astype(F32)
        ).astype(BF)
        push(part.at[j, s, xp], land.at[j, 0, k], l_recv.at[j, 0], dev_xp)
        arrived(relm.at[j, k], p_recv.at[j, 1])
        part[j, s, xm, :, cut:] = (
            part[j, s, xm, :, cut:].astype(F32) + relm[j, k].astype(F32)
        ).astype(BF)
        push(part.at[j, s, xm], land.at[j, 1, k], l_recv.at[j, 1], dev_xm)

    def line_sum(j, z, k):
        return part[j, z, x].astype(F32) + land[j, 0, k].astype(F32) + land[j, 1, k].astype(F32)

    def pair_last(j):
        k = slot(j)
        arrived(land.at[j, 0, k], l_recv.at[j, 0])
        arrived(land.at[j, 1, k], l_recv.at[j, 1])
        if KINDS[j] == "z":
            return
        zs[j] = line_sum(j, 1 - zl, 1 - zl).astype(BF)
        push(zs.at[j], zr.at[j], z_recv.at[j], dev_z)

    def share(j, z, xx, targets):
        piece = hid.at[j, z, xx]
        for dev in targets:
            push(piece, piece, h_recv.at[j, z, xx], dev)

    def element(j):
        if KINDS[j] == "z":
            total = line_sum(j, zl, 0)
        else:
            arrived(zr.at[j], z_recv.at[j])
            total = line_sum(j, zl, zl) + zr[j].astype(F32)
        gate, up, dh = total[:, :f], total[:, f : 2 * f], total[:, 2 * f :]
        sig = jax.nn.sigmoid(gate)
        act = gate * sig
        hid[j, zl, x, :, 0:f] = (act * up).astype(BF)
        hid[j, zl, x, :, f : 2 * f] = (dh * up * sig * (1.0 + gate * (1.0 - sig))).astype(BF)
        hid[j, zl, x, :, 2 * f : 3 * f] = (dh * act).astype(BF)
        share(j, zl, x, [dev_xp, dev_xm, dev_z])

    def pair_share(j):
        if KINDS[j] == "z":
            return
        arrived(hid.at[j, 1 - zl, x], h_recv.at[j, 1 - zl, x])
        share(j, 1 - zl, x, [dev_xp, dev_xm])

    def line_share(j):
        s = span(j)
        rows = [zl] if KINDS[j] == "z" else [0, 1]
        for src, half, dev, n in ((xm, pl.ds(0, cut), dev_xp, 0), (xp, pl.ds(cut, 3 * f - cut), dev_xm, 1)):
            for z in rows:
                arrived(hid.at[j, z, src], h_recv.at[j, z, src])
            piece = hid.at[j, s, src, :, half]
            push(piece, piece, h2_recv.at[j, n], dev)
            if KINDS[j] == "z":
                share(j, zl, src, [dev_z])

    def far_share(j):
        arrived(hid.at[j, span(j), x2, :, :cut], h2_recv.at[j, 0])
        arrived(hid.at[j, span(j), x2, :, cut:], h2_recv.at[j, 1])
        if KINDS[j] == "z":
            share(j, zl, x2, [dev_z])

    def back(j):
        if KINDS[j] == "z":
            for xx in range(4):
                arrived(hid.at[j, 1 - zl, xx], h_recv.at[j, 1 - zl, xx])
        dg = hid[j, :, :, :, f : 2 * f].reshape(8 * G, f)
        du = hid[j, :, :, :, 2 * f : 3 * f].reshape(8 * G, f)
        gt[j] = (nt(dg, gw[...]) + nt(du, uw[...])).astype(BF).reshape(2, 4, G, d)
        push(gt.at[j, 1 - core], sib.at[j], s_recv.at[j], dev_core)
        hid_t[:, j * 8 * G : (j + 1) * 8 * G] = hid[j, :, :, :, 0:f].reshape(8 * G, f).T

    def core_sum(j):
        arrived(sib.at[j], s_recv.at[j])
        if j > 0:
            ysend[j - 1] = (gt[j, core].astype(F32) + sib[j].astype(F32)).astype(BF)
            push(ysend.at[j - 1], yland.at[j - 1], y_recv.at[j - 1], dev_y[ORDER[j] - 1])

    def y_sum():
        total = gt[0, core].astype(F32) + sib[0].astype(F32)
        for k in range(3):
            arrived(yland.at[k], y_recv.at[k])
            total = total + yland[k].astype(F32)
        zsend[...] = total.astype(BF)
        for k in (1, 0, 2):
            push(zsend.at[(zh + k + 1) % 4], zland.at[k], zh_recv.at[k], dev_zh[k])

    def z_sum():
        total = zsend[zh].astype(F32)
        for k in range(3):
            arrived(zland.at[k], zh_recv.at[k])
            total = total + zland[k].astype(F32)
        o_tok[...] = total.astype(BF)

    outs = []

    def weight_grad(lhs, rhs, stage, out, sem):
        rows = 256 if lhs.shape[0] % 256 == 0 else 128
        for m in range(0, lhs.shape[0], rows):
            stage[m : m + rows, :] = nn(lhs[m : m + rows, :], rhs).astype(BF)
        cp = pltpu.make_async_copy(stage, out, loc.at[sem])
        cp.start()
        outs.append(cp)

    def grad_down():
        weight_grad(hid_t, w_st[...], od, o_down, 5)

    def grad_gate():
        weight_grad(tok_t, hid[:, :, :, :, f : 2 * f].reshape(TOKENS, f), og, o_gate, 6)

    def grad_up():
        weight_grad(tok_t, hid[:, :, :, :, 2 * f : 3 * f].reshape(TOKENS, f), ou, o_up, 7)

    gather_own()
    multiply(0)
    gather_far(1)
    gather_far(2)
    pair_first(0)
    multiply(1)
    forward(0)
    gather_far(3)
    multiply(2)
    pair_first(1)
    forward(1)
    multiply(3)
    pair_last(0)
    pair_first(2)
    forward(2)
    element(0)
    pair_last(1)
    pair_first(3)
    forward(3)
    pair_share(0)
    element(1)
    pair_last(2)
    line_share(0)
    pair_share(1)
    element(2)
    pair_last(3)
    far_share(0)
    line_share(1)
    pair_share(2)
    element(3)
    back(0)
    far_share(1)
    line_share(2)
    pair_share(3)
    core_sum(0)
    back(1)
    far_share(2)
    line_share(3)
    core_sum(1)
    back(2)
    far_share(3)
    core_sum(2)
    back(3)
    grad_down()
    core_sum(3)
    grad_gate()
    y_sum()
    grad_up()
    z_sum()
    for cp in outs:
        cp.wait()
    for cp in sent:
        cp.wait_send()


SENDS = 128


def per_device(tokens, grad_output, gate_weight, up_weight, down_weight, segment_ids):
    d, f = gate_weight.shape
    cut = (3 * f // 256 + 1) * 128
    vm, dma = pltpu.VMEM, pltpu.SemaphoreType.DMA
    whole = pl.BlockSpec(memory_space=pltpu.VMEM)
    hbm = pl.BlockSpec(memory_space=pl.ANY)
    return pl.pallas_call(
        kernel,
        out_shape=(
            jax.ShapeDtypeStruct(tokens.shape, BF),
            jax.ShapeDtypeStruct(gate_weight.shape, BF),
            jax.ShapeDtypeStruct(up_weight.shape, BF),
            jax.ShapeDtypeStruct(down_weight.shape, BF),
        ),
        in_specs=[hbm, hbm, whole, hbm, hbm, hbm],
        out_specs=(whole, hbm, hbm, hbm),
        scratch_shapes=[
            vm((4, 2, 4, 2, G, d), BF),
            vm((G, d), BF),
            vm((d, f), BF),
            vm((d, f), BF),
            vm((f, d), BF),
            vm((4, 2, 4, G, 3 * f), BF),
            vm((4, 2, G, cut), BF),
            vm((4, 2, G, 3 * f - cut), BF),
            vm((4, 2, 2, G, 3 * f), BF),
            vm((4, G, 3 * f), BF),
            vm((4, G, 3 * f), BF),
            vm((4, 4, G, 3 * f), BF),
            vm((4, 2, 4, G, 3 * f), BF),
            vm((4, 2, 4, G, d), BF),
            vm((4, 4, G, d), BF),
            vm((3, 4, G, d), BF),
            vm((3, 4, G, d), BF),
            vm((4, G, d), BF),
            vm((3, G, d), BF),
            vm((G, d), F32),
            vm((d, TOKENS), BF),
            vm((f, TOKENS), BF),
            vm((TOKENS, d), BF),
            vm((d, f), BF),
            vm((d, f), BF),
            vm((f, d), BF),
            dma((SENDS,)),
            dma((8,)),
            dma((4, 2, 4)),
            dma((4, 2)),
            dma((4, 2)),
            dma((4,)),
            dma((4, 2, 4)),
            dma((4, 2)),
            dma((4,)),
            dma((3,)),
            dma((3,)),
        ],
        compiler_params=pltpu.CompilerParams(
            collective_id=0, has_side_effects=True, vmem_limit_bytes=56 << 20
        ),
    )(tokens, grad_output, segment_ids.reshape(1, TOKENS), gate_weight, up_weight, down_weight)


def solution(mesh):
    in_specs = (
        P("col", "row"),
        P("col", "row"),
        P("row", "col"),
        P("row", "col"),
        P("col", "row"),
        P(),
    )
    out_specs = (P("col", "row"), P("row", "col"), P("row", "col"), P("col", "row"))
    return jax.shard_map(
        per_device, mesh=mesh, in_specs=in_specs, out_specs=out_specs, check_vma=False
    )
```

```python
import functools

import jax
import jax.numpy as jnp
from jax import lax
from jax.experimental import pallas as pl
from jax.experimental.pallas import tpu as pltpu
from jax.sharding import PartitionSpec as P

MESH = pl.DeviceIdType.MESH
BF = jnp.bfloat16
F32 = jnp.float32
TOKENS = 512
SEGS = 64
G = 16
ORDER = (0, 1, 3, 2)
X_SHARE, ALL = 12, 21


def nn(a, b):
    return jnp.dot(a, b, preferred_element_type=F32)


def nt(a, b):
    return lax.dot_general(a, b, (((1,), (1,)), ((), ())), preferred_element_type=F32)


def widths(f):
    wx = 3 * f * X_SHARE // ALL
    wz = 3 * f - wx
    return wx, wz, (wx // 256) * 128, ((wz + 128) // 256) * 128


def kernel(
    tokens, grad, ids, gate_w, up_w, down_w,
    o_tok, o_gate, o_up, o_down,
    tw, gst, gw, uw, dw, px, pz, rpx, rmx, rpz, rmz, lx, lz, zs, zr, zbig, hx, hz,
    gt, sib, ysend, yland, zsend, zland, tok_t, hid_t, w_st,
    ssem, loc, a_recv, rx_recv, rz_recv, lx_recv, lz_recv, zr_recv, zb_recv,
    hx_recv, hz_recv, gx_recv, gz_recv, s_recv, y_recv, zh_recv,
):
    d, f = gw.shape
    wx, wz, cx, cz = widths(f)
    r, c = lax.axis_index("row"), lax.axis_index("col")
    x, zl = r % 4, r // 4
    core, zh, y = c % 2, (c // 2) % 4, c // 8
    xp, xm, x2 = (x + 1) % 4, (x + 3) % 4, (x + 2) % 4

    def at(x=x, zl=zl, y=y, zh=zh, core=core):
        return {"row": zl * 4 + x, "col": (y * 4 + zh) * 2 + core}

    dev_xp, dev_xm, dev_z, dev_core = at(x=xp), at(x=xm), at(zl=1 - zl), at(core=1 - core)
    dev_zh = [at(zh=(zh + k) % 4) for k in (1, 2, 3)]
    dev_y = [at(y=(y + k) % 4) for k in (1, 2, 3)]
    partners = [dev_xp, dev_xm, dev_z, dev_core] + dev_zh + dev_y

    barrier = pltpu.get_barrier_semaphore()
    for p in partners:
        pl.semaphore_signal(barrier, inc=1, device_id=p, device_id_type=MESH)

    first = [
        pltpu.make_async_copy(tokens, tw.at[zh, core, y, 0], loc.at[0]),
        pltpu.make_async_copy(grad, gst, loc.at[1]),
    ]
    weights = [
        pltpu.make_async_copy(gate_w, gw, loc.at[2]),
        pltpu.make_async_copy(up_w, uw, loc.at[3]),
        pltpu.make_async_copy(down_w, dw, loc.at[4]),
    ]
    for cp in first + weights:
        cp.start()

    idr = jnp.broadcast_to(ids[...].astype(F32), (G, TOKENS))
    lane = lax.broadcasted_iota(jnp.int32, (G, TOKENS), 1)
    row = lax.broadcasted_iota(jnp.int32, (G, TOKENS), 0)
    mine = jnp.sum(jnp.where(lane == c * G + row, idr, 0.0), axis=1, keepdims=True)
    count = jnp.sum(jnp.where(idr == mine, 1.0, 0.0), axis=1, keepdims=True)
    weight = (TOKENS / SEGS) / count
    for cp in first:
        cp.wait()
    tw[zh, core, y, 1] = (gst[...].astype(F32) * weight).astype(BF)
    pl.semaphore_wait(barrier, len(partners))

    sent = []

    def push(src, dst, recv, dev):
        cp = pltpu.make_async_remote_copy(
            src_ref=src, dst_ref=dst, send_sem=ssem.at[len(sent)], recv_sem=recv,
            device_id=dev, device_id_type=MESH,
        )
        cp.start()
        sent.append(cp)

    def arrived(ref, recv):
        pltpu.make_async_remote_copy(
            src_ref=ref, dst_ref=ref, send_sem=ssem.at[0], recv_sem=recv,
            device_id=dev_core, device_id_type=MESH,
        ).wait_recv()

    def spread(hh, targets):
        piece = tw.at[hh, core, y]
        for dev in targets:
            push(piece, piece, a_recv.at[hh, core, y], dev)

    def gather_own():
        spread(zh, [dev_zh[0], dev_zh[2], dev_zh[1]])
        spread(zh, [dev_y[0], dev_y[2], dev_y[1], dev_core])

    def gather_far(j):
        hh = (zh + ORDER[j]) % 4
        arrived(tw.at[hh, core, y], a_recv.at[hh, core, y])
        spread(hh, [dev_y[0], dev_y[2], dev_y[1], dev_core])

    def gather_line(j):
        hh = (zh + ORDER[j]) % 4
        for k in (1, 3, 2):
            piece = tw.at[hh, core, (y + k) % 4]
            arrived(piece, a_recv.at[hh, core, (y + k) % 4])
            push(piece, piece, a_recv.at[hh, core, (y + k) % 4], dev_core)

    def multiply(j):
        hh = (zh + ORDER[j]) % 4
        for yy in range(4):
            arrived(tw.at[hh, 1 - core, yy], a_recv.at[hh, 1 - core, yy])
        t = tw[hh, :, :, 0].reshape(8 * G, d)
        w = tw[hh, :, :, 1].reshape(8 * G, d)
        if j == 0:
            for cp in weights:
                cp.wait()
        p = nn(t, gw[...]).astype(BF).reshape(2, 4, G, f)
        px[j, :, :, :, 0:f] = p
        p = nn(t, uw[...]).astype(BF).reshape(2, 4, G, f)
        px[j, :, :, :, f:wx] = p[:, :, :, : wx - f]
        relay_x(j)
        pz[j, :, :, :, : 2 * f - wx] = p[:, :, :, wx - f :]
        pz[j, :, :, :, 2 * f - wx :] = nt(w, dw[...]).astype(BF).reshape(2, 4, G, f)
        push(pz.at[j, 1 - zl], zbig.at[j], zb_recv.at[j], dev_z)
        tok_t[:, j * 8 * G : (j + 1) * 8 * G] = t.T
        w_st[j * 8 * G : (j + 1) * 8 * G, :] = w

    def relay_x(j):
        push(px.at[j, :, x2, :, :cx], rpx.at[j], rx_recv.at[j, 0], dev_xp)
        push(px.at[j, :, x2, :, cx:], rmx.at[j], rx_recv.at[j, 1], dev_xm)
        push(px.at[j, :, xp, :, cx:], lx.at[j, 0, :, :, cx:], lx_recv.at[j, 0, 1], dev_xp)
        push(px.at[j, :, xm, :, :cx], lx.at[j, 1, :, :, :cx], lx_recv.at[j, 1, 0], dev_xm)

    def relay_z(j):
        push(pz.at[j, zl, x2, :, :cz], rpz.at[j], rz_recv.at[j, 0], dev_xp)
        push(pz.at[j, zl, x2, :, cz:], rmz.at[j], rz_recv.at[j, 1], dev_xm)
        push(pz.at[j, zl, xp, :, cz:], lz.at[j, 0, :, cz:], lz_recv.at[j, 0, 1], dev_xp)
        push(pz.at[j, zl, xm, :, :cz], lz.at[j, 1, :, :cz], lz_recv.at[j, 1, 0], dev_xm)

    def pair_first(j):
        arrived(zbig.at[j], zb_recv.at[j])
        pz[j, zl] = (pz[j, zl].astype(F32) + zbig[j].astype(F32)).astype(BF)
        relay_z(j)

    def forward_x(j):
        arrived(rpx.at[j], rx_recv.at[j, 0])
        rpx[j] = (px[j, :, xp, :, :cx].astype(F32) + rpx[j].astype(F32)).astype(BF)
        push(rpx.at[j], lx.at[j, 0, :, :, :cx], lx_recv.at[j, 0, 0], dev_xp)
        arrived(rmx.at[j], rx_recv.at[j, 1])
        rmx[j] = (px[j, :, xm, :, cx:].astype(F32) + rmx[j].astype(F32)).astype(BF)
        push(rmx.at[j], lx.at[j, 1, :, :, cx:], lx_recv.at[j, 1, 1], dev_xm)

    def forward_z(j):
        arrived(rpz.at[j], rz_recv.at[j, 0])
        rpz[j] = (pz[j, zl, xp, :, :cz].astype(F32) + rpz[j].astype(F32)).astype(BF)
        push(rpz.at[j], lz.at[j, 0, :, :cz], lz_recv.at[j, 0, 0], dev_xp)
        arrived(rmz.at[j], rz_recv.at[j, 1])
        rmz[j] = (pz[j, zl, xm, :, cz:].astype(F32) + rmz[j].astype(F32)).astype(BF)
        push(rmz.at[j], lz.at[j, 1, :, cz:], lz_recv.at[j, 1, 1], dev_xm)

    def sum_x(j, z):
        return px[j, z, x].astype(F32) + lx[j, 0, z].astype(F32) + lx[j, 1, z].astype(F32)

    def pair_last(j):
        for n in range(2):
            arrived(lx.at[j, n, :, :, :cx], lx_recv.at[j, n, 0])
            arrived(lx.at[j, n, :, :, cx:], lx_recv.at[j, n, 1])
        zs[j] = sum_x(j, 1 - zl).astype(BF)
        push(zs.at[j], zr.at[j], zr_recv.at[j], dev_z)

    def share_x(j, z, xx, targets):
        piece = hx.at[j, z, xx]
        for dev in targets:
            push(piece, piece, hx_recv.at[j, z, xx], dev)

    def share_z(j, xx, targets):
        piece = hz.at[j, zl, xx]
        for dev in targets:
            push(piece, piece, hz_recv.at[j, zl, xx], dev)

    def element(j):
        for n in range(2):
            arrived(lz.at[j, n, :, :cz], lz_recv.at[j, n, 0])
            arrived(lz.at[j, n, :, cz:], lz_recv.at[j, n, 1])
        arrived(zr.at[j], zr_recv.at[j])
        tx = sum_x(j, zl) + zr[j].astype(F32)
        tz = pz[j, zl, x].astype(F32) + lz[j, 0].astype(F32) + lz[j, 1].astype(F32)
        gate, dh = tx[:, :f], tz[:, 2 * f - wx :]
        up = jnp.concatenate([tx[:, f:], tz[:, : 2 * f - wx]], axis=1)
        sig = jax.nn.sigmoid(gate)
        act = gate * sig
        hx[j, zl, x, :, 0:f] = (act * up).astype(BF)
        d_gate = (dh * up * sig * (1.0 + gate * (1.0 - sig))).astype(BF)
        hx[j, zl, x, :, f:wx] = d_gate[:, : wx - f]
        hz[j, zl, x, :, : 2 * f - wx] = d_gate[:, wx - f :]
        hz[j, zl, x, :, 2 * f - wx :] = (dh * act).astype(BF)
        share_x(j, zl, x, [dev_z, dev_xp, dev_xm])
        share_z(j, x, [dev_xp, dev_xm, dev_z])

    def pair_share(j):
        arrived(hx.at[j, 1 - zl, x], hx_recv.at[j, 1 - zl, x])
        share_x(j, 1 - zl, x, [dev_xp, dev_xm])

    def line_share_x(j):
        for src, half, dev, n in ((xm, slice(0, cx), dev_xp, 0), (xp, slice(cx, wx), dev_xm, 1)):
            for z in range(2):
                arrived(hx.at[j, z, src], hx_recv.at[j, z, src])
            piece = hx.at[j, :, src, :, half]
            push(piece, piece, gx_recv.at[j, n], dev)

    def line_share_z(j):
        for src, half, dev, n in ((xm, slice(0, cz), dev_xp, 0), (xp, slice(cz, wz), dev_xm, 1)):
            arrived(hz.at[j, zl, src], hz_recv.at[j, zl, src])
            piece = hz.at[j, zl, src, :, half]
            push(piece, piece, gz_recv.at[j, n], dev)
            share_z(j, src, [dev_z])

    def far_share(j):
        arrived(hz.at[j, zl, x2, :, :cz], gz_recv.at[j, 0])
        arrived(hz.at[j, zl, x2, :, cz:], gz_recv.at[j, 1])
        share_z(j, x2, [dev_z])

    def d_gate_of(j):
        left = hx[j, :, :, :, f:wx]
        right = hz[j, :, :, :, : 2 * f - wx]
        return jnp.concatenate([left, right], axis=-1).reshape(8 * G, f)

    def d_up_of(j):
        return hz[j, :, :, :, 2 * f - wx :].reshape(8 * G, f)

    def back(j):
        arrived(hx.at[j, :, x2, :, :cx], gx_recv.at[j, 0])
        arrived(hx.at[j, :, x2, :, cx:], gx_recv.at[j, 1])
        for xx in range(4):
            arrived(hz.at[j, 1 - zl, xx], hz_recv.at[j, 1 - zl, xx])
        back_sum = nt(d_gate_of(j), gw[...]) + nt(d_up_of(j), uw[...])
        gt[j] = back_sum.astype(BF).reshape(2, 4, G, d)
        push(gt.at[j, 1 - core], sib.at[j], s_recv.at[j], dev_core)
        hid_t[:, j * 8 * G : (j + 1) * 8 * G] = hx[j, :, :, :, 0:f].reshape(8 * G, f).T

    def core_sum(j):
        arrived(sib.at[j], s_recv.at[j])
        ysend[j] = (gt[j, core].astype(F32) + sib[j].astype(F32)).astype(BF)
        for k in (1, 0, 2):
            push(ysend.at[j, (y + k + 1) % 4], yland.at[j, k], y_recv.at[j, k], dev_y[k])

    def y_total(j):
        total = gt[j, core, y].astype(F32) + sib[j, y].astype(F32)
        for k in range(3):
            arrived(yland.at[j, k], y_recv.at[j, k])
            total = total + yland[j, k].astype(F32)
        return total

    def y_sum(j):
        zsend[j - 1] = y_total(j).astype(BF)
        push(zsend.at[j - 1], zland.at[j - 1], zh_recv.at[j - 1], dev_zh[ORDER[j] - 1])

    def finish():
        total = y_total(0)
        for k in range(3):
            arrived(zland.at[k], zh_recv.at[k])
            total = total + zland[k].astype(F32)
        o_tok[...] = total.astype(BF)

    def weight_grad(lhs, rhs, out):
        rows = 256 if lhs.shape[0] % 256 == 0 else 128
        for m in range(0, lhs.shape[0], rows):
            out[m : m + rows, :] = nn(lhs[m : m + rows, :], rhs).astype(BF)

    def grad_down():
        weight_grad(hid_t, w_st[...], o_down)

    def grad_gate():
        weight_grad(tok_t, jnp.concatenate([d_gate_of(j) for j in range(4)], axis=0), o_gate)

    def grad_up():
        weight_grad(tok_t, jnp.concatenate([d_up_of(j) for j in range(4)], axis=0), o_up)

    gather_own()
    gather_far(2)
    gather_line(0)
    gather_far(1)
    multiply(0)
    gather_line(2)
    gather_far(3)
    forward_x(0)
    gather_line(1)
    multiply(2)
    pair_first(0)
    gather_line(3)
    multiply(1)
    forward_x(2)
    multiply(3)
    pair_first(2)
    forward_x(1)
    pair_last(2)
    pair_first(1)
    forward_z(2)
    forward_x(3)
    pair_last(0)
    forward_z(0)
    pair_last(1)
    forward_z(1)
    pair_first(3)
    element(2)
    pair_last(3)
    forward_z(3)
    element(1)
    pair_share(2)
    line_share_z(2)
    element(3)
    line_share_z(1)
    pair_share(1)
    line_share_x(2)
    far_share(2)
    far_share(1)
    pair_share(3)
    line_share_z(3)
    line_share_x(1)
    element(0)
    back(2)
    far_share(3)
    line_share_x(3)
    back(1)
    pair_share(0)
    line_share_z(0)
    core_sum(2)
    back(3)
    line_share_x(0)
    far_share(0)
    core_sum(1)
    core_sum(3)
    y_sum(2)
    back(0)
    y_sum(1)
    grad_down()
    y_sum(3)
    core_sum(0)
    grad_gate()
    grad_up()
    finish()
    for cp in sent:
        cp.wait_send()


SENDS = 192
VMEM_LIMIT = 58 << 20


def per_device(tokens, grad_output, gate_weight, up_weight, down_weight, segment_ids):
    d, f = gate_weight.shape
    wx, wz, cx, cz = widths(f)
    vm, dma = pltpu.VMEM, pltpu.SemaphoreType.DMA
    whole = pl.BlockSpec(memory_space=pltpu.VMEM)
    hbm = pl.BlockSpec(memory_space=pl.ANY)
    return pl.pallas_call(
        kernel,
        out_shape=(
            vm(tokens.shape, BF),
            vm(gate_weight.shape, BF),
            vm(up_weight.shape, BF),
            vm(down_weight.shape, BF),
        ),
        in_specs=[hbm, hbm, whole, hbm, hbm, hbm],
        out_specs=(whole, whole, whole, whole),
        scratch_shapes=[
            vm((4, 2, 4, 2, G, d), BF),
            vm((G, d), BF),
            vm((d, f), BF),
            vm((d, f), BF),
            vm((f, d), BF),
            vm((4, 2, 4, G, wx), BF),
            vm((4, 2, 4, G, wz), BF),
            vm((4, 2, G, cx), BF),
            vm((4, 2, G, wx - cx), BF),
            vm((4, G, cz), BF),
            vm((4, G, wz - cz), BF),
            vm((4, 2, 2, G, wx), BF),
            vm((4, 2, G, wz), BF),
            vm((4, G, wx), BF),
            vm((4, G, wx), BF),
            vm((4, 4, G, wz), BF),
            vm((4, 2, 4, G, wx), BF),
            vm((4, 2, 4, G, wz), BF),
            vm((4, 2, 4, G, d), BF),
            vm((4, 4, G, d), BF),
            vm((4, 4, G, d), BF),
            vm((4, 3, G, d), BF),
            vm((3, G, d), BF),
            vm((3, G, d), BF),
            vm((d, TOKENS), BF),
            vm((f, TOKENS), BF),
            vm((TOKENS, d), BF),
            dma((SENDS,)),
            dma((5,)),
            dma((4, 2, 4)),
            dma((4, 2)),
            dma((4, 2)),
            dma((4, 2, 2)),
            dma((4, 2, 2)),
            dma((4,)),
            dma((4,)),
            dma((4, 2, 4)),
            dma((4, 2, 4)),
            dma((4, 2)),
            dma((4, 2)),
            dma((4,)),
            dma((4, 3)),
            dma((3,)),
        ],
        compiler_params=pltpu.CompilerParams(
            collective_id=0, has_side_effects=True, vmem_limit_bytes=VMEM_LIMIT
        ),
    )(tokens, grad_output, segment_ids.reshape(1, TOKENS), gate_weight, up_weight, down_weight)


def solution(mesh):
    in_specs = (
        P("col", "row"),
        P("col", "row"),
        P("row", "col"),
        P("row", "col"),
        P("col", "row"),
        P(),
    )
    out_specs = (P("col", "row"), P("row", "col"), P("row", "col"), P("col", "row"))
    return jax.shard_map(
        per_device, mesh=mesh, in_specs=in_specs, out_specs=out_specs, check_vma=False
    )
```

```python
import functools

import jax
import jax.numpy as jnp
from jax import lax
from jax.experimental import pallas as pl
from jax.experimental.pallas import tpu as pltpu
from jax.sharding import PartitionSpec as P

MESH = pl.DeviceIdType.MESH
BF = jnp.bfloat16
F32 = jnp.float32
TOKENS = 512
SEGS = 64
G = 16
ORDER = (0, 1, 3, 2)
X_SHARE, ALL = 12, 21


def nn(a, b):
    return jnp.dot(a, b, preferred_element_type=F32)


def nt(a, b):
    return lax.dot_general(a, b, (((1,), (1,)), ((), ())), preferred_element_type=F32)


def widths(f):
    wx = 3 * f * X_SHARE // ALL
    wz = 3 * f - wx
    return wx, wz, (wx // 256) * 128, ((wz + 128) // 256) * 128


def kernel(
    tokens, grad, ids, gate_w, up_w, down_w,
    o_tok, o_gate, o_up, o_down,
    tw, gst, idv, gw, uw, dw, px, pz, rpx, rmx, rpz, rmz, lx, lz, zs, zr, zbig, hx, hz,
    gt, sib, ysend, yland, ycross, zsend, zland, tok_t, hid_t, w_st,
    ssem, loc, a_recv, rx_recv, rz_recv, lx_recv, lz_recv, zr_recv, zb_recv,
    hx_recv, hz_recv, gx_recv, gz_recv, s_recv, y_recv, yc_recv, zh_recv,
):
    d, f = gw.shape
    wx, wz, cx, cz = widths(f)
    r, c = lax.axis_index("row"), lax.axis_index("col")
    x, zl = r % 4, r // 4
    core, zh, y = c % 2, (c // 2) % 4, c // 8
    xp, xm, x2 = (x + 1) % 4, (x + 3) % 4, (x + 2) % 4

    def at(x=x, zl=zl, y=y, zh=zh, core=core):
        return {"row": zl * 4 + x, "col": (y * 4 + zh) * 2 + core}

    dev_xp, dev_xm, dev_z, dev_core = at(x=xp), at(x=xm), at(zl=1 - zl), at(core=1 - core)
    dev_zh = [at(zh=(zh + k) % 4) for k in (1, 2, 3)]
    dev_y = [at(y=(y + k) % 4) for k in (1, 2, 3)]
    dev_yc = [at(y=(y + k) % 4, core=1 - core) for k in (1, 2, 3)]
    partners = [dev_xp, dev_xm, dev_z, dev_core] + dev_zh + dev_y + dev_yc

    barrier = pltpu.get_barrier_semaphore()
    for p in partners:
        pl.semaphore_signal(barrier, inc=1, device_id=p, device_id_type=MESH)

    first = [
        pltpu.make_async_copy(tokens, tw.at[zh, core, y, 0], loc.at[0]),
        pltpu.make_async_copy(grad, gst, loc.at[1]),
        pltpu.make_async_copy(ids, idv, loc.at[5]),
    ]
    weights = [
        pltpu.make_async_copy(gate_w, gw, loc.at[2]),
        pltpu.make_async_copy(up_w, uw, loc.at[3]),
        pltpu.make_async_copy(down_w, dw, loc.at[4]),
    ]
    for cp in first + weights:
        cp.start()

    for cp in first:
        cp.wait()
    idr = jnp.broadcast_to(idv[...].astype(F32), (G, TOKENS))
    lane = lax.broadcasted_iota(jnp.int32, (G, TOKENS), 1)
    row = lax.broadcasted_iota(jnp.int32, (G, TOKENS), 0)
    mine = jnp.sum(jnp.where(lane == c * G + row, idr, 0.0), axis=1, keepdims=True)
    count = jnp.sum(jnp.where(idr == mine, 1.0, 0.0), axis=1, keepdims=True)
    weight = (TOKENS / SEGS) / count
    tw[zh, core, y, 1] = (gst[...].astype(F32) * weight).astype(BF)
    pl.semaphore_wait(barrier, len(partners))

    sent = []

    def push(src, dst, recv, dev):
        cp = pltpu.make_async_remote_copy(
            src_ref=src, dst_ref=dst, send_sem=ssem.at[len(sent)], recv_sem=recv,
            device_id=dev, device_id_type=MESH,
        )
        cp.start()
        sent.append(cp)

    def arrived(ref, recv):
        pltpu.make_async_remote_copy(
            src_ref=ref, dst_ref=ref, send_sem=ssem.at[0], recv_sem=recv,
            device_id=dev_core, device_id_type=MESH,
        ).wait_recv()

    def spread(hh, targets):
        piece = tw.at[hh, core, y]
        for dev in targets:
            push(piece, piece, a_recv.at[hh, core, y], dev)

    def gather_own():
        spread(zh, [dev_zh[0], dev_zh[2], dev_zh[1]])
        spread(zh, [dev_y[0], dev_y[2], dev_y[1], dev_core])

    def gather_far(j):
        hh = (zh + ORDER[j]) % 4
        arrived(tw.at[hh, core, y], a_recv.at[hh, core, y])
        spread(hh, [dev_y[0], dev_y[2], dev_y[1], dev_core])

    def gather_line(j):
        hh = (zh + ORDER[j]) % 4
        for k in (1, 3, 2):
            piece = tw.at[hh, core, (y + k) % 4]
            arrived(piece, a_recv.at[hh, core, (y + k) % 4])
            push(piece, piece, a_recv.at[hh, core, (y + k) % 4], dev_core)

    def multiply(j):
        hh = (zh + ORDER[j]) % 4
        for yy in range(4):
            arrived(tw.at[hh, 1 - core, yy], a_recv.at[hh, 1 - core, yy])
        t = tw[hh, :, :, 0].reshape(8 * G, d)
        w = tw[hh, :, :, 1].reshape(8 * G, d)
        if j == 0:
            for cp in weights:
                cp.wait()
        p = nn(t, gw[...]).astype(BF).reshape(2, 4, G, f)
        px[j, :, :, :, 0:f] = p
        p = nn(t, uw[...]).astype(BF).reshape(2, 4, G, f)
        px[j, :, :, :, f:wx] = p[:, :, :, : wx - f]
        relay_x(j)
        pz[j, :, :, :, : 2 * f - wx] = p[:, :, :, wx - f :]
        pz[j, :, :, :, 2 * f - wx :] = nt(w, dw[...]).astype(BF).reshape(2, 4, G, f)
        push(pz.at[j, 1 - zl], zbig.at[j], zb_recv.at[j], dev_z)
        tok_t[:, j * 8 * G : (j + 1) * 8 * G] = t.T
        w_st[j * 8 * G : (j + 1) * 8 * G, :] = w

    def relay_x(j):
        push(px.at[j, :, x2, :, :cx], rpx.at[j], rx_recv.at[j, 0], dev_xp)
        push(px.at[j, :, x2, :, cx:], rmx.at[j], rx_recv.at[j, 1], dev_xm)
        push(px.at[j, :, xp, :, cx:], lx.at[j, 0, :, :, cx:], lx_recv.at[j, 0, 1], dev_xp)
        push(px.at[j, :, xm, :, :cx], lx.at[j, 1, :, :, :cx], lx_recv.at[j, 1, 0], dev_xm)

    def relay_z(j):
        push(pz.at[j, zl, x2, :, :cz], rpz.at[j], rz_recv.at[j, 0], dev_xp)
        push(pz.at[j, zl, x2, :, cz:], rmz.at[j], rz_recv.at[j, 1], dev_xm)
        push(pz.at[j, zl, xp, :, cz:], lz.at[j, 0, :, cz:], lz_recv.at[j, 0, 1], dev_xp)
        push(pz.at[j, zl, xm, :, :cz], lz.at[j, 1, :, :cz], lz_recv.at[j, 1, 0], dev_xm)

    def pair_first(j):
        arrived(zbig.at[j], zb_recv.at[j])
        pz[j, zl] = (pz[j, zl].astype(F32) + zbig[j].astype(F32)).astype(BF)
        relay_z(j)

    def forward_x(j):
        arrived(rpx.at[j], rx_recv.at[j, 0])
        rpx[j] = (px[j, :, xp, :, :cx].astype(F32) + rpx[j].astype(F32)).astype(BF)
        push(rpx.at[j], lx.at[j, 0, :, :, :cx], lx_recv.at[j, 0, 0], dev_xp)
        arrived(rmx.at[j], rx_recv.at[j, 1])
        rmx[j] = (px[j, :, xm, :, cx:].astype(F32) + rmx[j].astype(F32)).astype(BF)
        push(rmx.at[j], lx.at[j, 1, :, :, cx:], lx_recv.at[j, 1, 1], dev_xm)

    def forward_z(j):
        arrived(rpz.at[j], rz_recv.at[j, 0])
        rpz[j] = (pz[j, zl, xp, :, :cz].astype(F32) + rpz[j].astype(F32)).astype(BF)
        push(rpz.at[j], lz.at[j, 0, :, :cz], lz_recv.at[j, 0, 0], dev_xp)
        arrived(rmz.at[j], rz_recv.at[j, 1])
        rmz[j] = (pz[j, zl, xm, :, cz:].astype(F32) + rmz[j].astype(F32)).astype(BF)
        push(rmz.at[j], lz.at[j, 1, :, cz:], lz_recv.at[j, 1, 1], dev_xm)

    def sum_x(j, z):
        return px[j, z, x].astype(F32) + lx[j, 0, z].astype(F32) + lx[j, 1, z].astype(F32)

    def pair_last(j):
        for n in range(2):
            arrived(lx.at[j, n, :, :, :cx], lx_recv.at[j, n, 0])
            arrived(lx.at[j, n, :, :, cx:], lx_recv.at[j, n, 1])
        zs[j] = sum_x(j, 1 - zl).astype(BF)
        push(zs.at[j], zr.at[j], zr_recv.at[j], dev_z)

    def share_x(j, z, xx, targets):
        piece = hx.at[j, z, xx]
        for dev in targets:
            push(piece, piece, hx_recv.at[j, z, xx], dev)

    def share_z(j, xx, targets):
        piece = hz.at[j, zl, xx]
        for dev in targets:
            push(piece, piece, hz_recv.at[j, zl, xx], dev)

    def element(j):
        for n in range(2):
            arrived(lz.at[j, n, :, :cz], lz_recv.at[j, n, 0])
            arrived(lz.at[j, n, :, cz:], lz_recv.at[j, n, 1])
        arrived(zr.at[j], zr_recv.at[j])
        tx = sum_x(j, zl) + zr[j].astype(F32)
        tz = pz[j, zl, x].astype(F32) + lz[j, 0].astype(F32) + lz[j, 1].astype(F32)
        gate, dh = tx[:, :f], tz[:, 2 * f - wx :]
        up = jnp.concatenate([tx[:, f:], tz[:, : 2 * f - wx]], axis=1)
        sig = jax.nn.sigmoid(gate)
        act = gate * sig
        hx[j, zl, x, :, 0:f] = (act * up).astype(BF)
        d_gate = (dh * up * sig * (1.0 + gate * (1.0 - sig))).astype(BF)
        hx[j, zl, x, :, f:wx] = d_gate[:, : wx - f]
        hz[j, zl, x, :, : 2 * f - wx] = d_gate[:, wx - f :]
        hz[j, zl, x, :, 2 * f - wx :] = (dh * act).astype(BF)
        share_x(j, zl, x, [dev_z, dev_xp, dev_xm])
        share_z(j, x, [dev_xp, dev_xm, dev_z])

    def pair_share(j):
        arrived(hx.at[j, 1 - zl, x], hx_recv.at[j, 1 - zl, x])
        share_x(j, 1 - zl, x, [dev_xp, dev_xm])

    def line_share_x(j):
        for src, half, dev, n in ((xm, slice(0, cx), dev_xp, 0), (xp, slice(cx, wx), dev_xm, 1)):
            for z in range(2):
                arrived(hx.at[j, z, src], hx_recv.at[j, z, src])
            piece = hx.at[j, :, src, :, half]
            push(piece, piece, gx_recv.at[j, n], dev)

    def line_share_z(j):
        for src, half, dev, n in ((xm, slice(0, cz), dev_xp, 0), (xp, slice(cz, wz), dev_xm, 1)):
            arrived(hz.at[j, zl, src], hz_recv.at[j, zl, src])
            piece = hz.at[j, zl, src, :, half]
            push(piece, piece, gz_recv.at[j, n], dev)
            share_z(j, src, [dev_z])

    def far_share(j):
        arrived(hz.at[j, zl, x2, :, :cz], gz_recv.at[j, 0])
        arrived(hz.at[j, zl, x2, :, cz:], gz_recv.at[j, 1])
        share_z(j, x2, [dev_z])

    def d_gate_of(j):
        left = hx[j, :, :, :, f:wx]
        right = hz[j, :, :, :, : 2 * f - wx]
        return jnp.concatenate([left, right], axis=-1).reshape(8 * G, f)

    def d_up_of(j):
        return hz[j, :, :, :, 2 * f - wx :].reshape(8 * G, f)

    def back(j):
        arrived(hx.at[j, :, x2, :, :cx], gx_recv.at[j, 0])
        arrived(hx.at[j, :, x2, :, cx:], gx_recv.at[j, 1])
        for xx in range(4):
            arrived(hz.at[j, 1 - zl, xx], hz_recv.at[j, 1 - zl, xx])
        back_sum = nt(d_gate_of(j), gw[...]) + nt(d_up_of(j), uw[...])
        gt[j] = back_sum.astype(BF).reshape(2, 4, G, d)
        if j > 0:
            push(gt.at[j, 1 - core], sib.at[j], s_recv.at[j], dev_core)
        else:
            for k in (1, 0, 2):
                yy = (y + k + 1) % 4
                push(gt.at[j, core, yy], yland.at[j, k], y_recv.at[j, k], dev_y[k])
                push(gt.at[j, 1 - core, yy], ycross.at[k], yc_recv.at[k], dev_yc[k])
            push(gt.at[j, 1 - core, y], sib.at[j, y], s_recv.at[j], dev_core)
        hid_t[:, j * 8 * G : (j + 1) * 8 * G] = hx[j, :, :, :, 0:f].reshape(8 * G, f).T

    def core_sum(j):
        arrived(sib.at[j], s_recv.at[j])
        ysend[j] = (gt[j, core].astype(F32) + sib[j].astype(F32)).astype(BF)
        for k in (1, 0, 2):
            push(ysend.at[j, (y + k + 1) % 4], yland.at[j, k], y_recv.at[j, k], dev_y[k])

    def y_total(j):
        total = gt[j, core, y].astype(F32) + sib[j, y].astype(F32)
        for k in range(3):
            arrived(yland.at[j, k], y_recv.at[j, k])
            total = total + yland[j, k].astype(F32)
        return total

    def y_sum(j):
        zsend[j - 1] = y_total(j).astype(BF)
        push(zsend.at[j - 1], zland.at[j - 1], zh_recv.at[j - 1], dev_zh[ORDER[j] - 1])

    def finish():
        arrived(sib.at[0, y], s_recv.at[0])
        total = y_total(0)
        for k in range(3):
            arrived(ycross.at[k], yc_recv.at[k])
            total = total + ycross[k].astype(F32)
        for k in range(3):
            arrived(zland.at[k], zh_recv.at[k])
            total = total + zland[k].astype(F32)
        o_tok[...] = total.astype(BF)

    def weight_grad(lhs, rhs, out):
        rows = 256 if lhs.shape[0] % 256 == 0 else 128
        for m in range(0, lhs.shape[0], rows):
            out[m : m + rows, :] = nn(lhs[m : m + rows, :], rhs).astype(BF)

    def grad_down():
        weight_grad(hid_t, w_st[...], o_down)

    def grad_gate():
        weight_grad(tok_t, jnp.concatenate([d_gate_of(j) for j in range(4)], axis=0), o_gate)

    def grad_up():
        weight_grad(tok_t, jnp.concatenate([d_up_of(j) for j in range(4)], axis=0), o_up)

    gather_own()
    gather_far(2)
    gather_line(0)
    gather_far(1)
    multiply(0)
    gather_line(2)
    gather_far(3)
    forward_x(0)
    gather_line(1)
    multiply(2)
    pair_first(0)
    gather_line(3)
    multiply(1)
    forward_x(2)
    multiply(3)
    pair_first(2)
    forward_x(1)
    pair_last(2)
    pair_first(1)
    forward_z(2)
    forward_x(3)
    pair_last(0)
    forward_z(0)
    pair_last(1)
    forward_z(1)
    pair_first(3)
    element(2)
    pair_last(3)
    forward_z(3)
    element(1)
    pair_share(2)
    line_share_z(2)
    element(3)
    line_share_z(1)
    pair_share(1)
    line_share_x(2)
    far_share(2)
    far_share(1)
    pair_share(3)
    line_share_z(3)
    line_share_x(1)
    element(0)
    back(2)
    far_share(3)
    line_share_x(3)
    back(1)
    pair_share(0)
    line_share_z(0)
    core_sum(2)
    back(3)
    line_share_x(0)
    far_share(0)
    core_sum(1)
    core_sum(3)
    y_sum(2)
    back(0)
    y_sum(1)
    grad_down()
    y_sum(3)
    grad_gate()
    grad_up()
    finish()
    for cp in sent:
        cp.wait_send()


SENDS = 192
VMEM_LIMIT = 58 << 20


def store(a, b, c, d, a_out, b_out, c_out, d_out, sems):
    pairs = ((a, a_out), (b, b_out), (c, c_out), (d, d_out))
    copies = [pltpu.make_async_copy(src, dst, sems.at[n]) for n, (src, dst) in enumerate(pairs)]
    for cp in copies:
        cp.start()
    for cp in copies:
        cp.wait()


def per_device(tokens, grad_output, gate_weight, up_weight, down_weight, segment_ids):
    d, f = gate_weight.shape
    wx, wz, cx, cz = widths(f)
    vm, dma = pltpu.VMEM, pltpu.SemaphoreType.DMA
    whole = pl.BlockSpec(memory_space=pltpu.VMEM)
    hbm = pl.BlockSpec(memory_space=pl.ANY)
    held = pl.pallas_call(
        kernel,
        out_shape=(
            vm(tokens.shape, BF),
            vm(gate_weight.shape, BF),
            vm(up_weight.shape, BF),
            vm(down_weight.shape, BF),
        ),
        in_specs=[hbm] * 6,
        out_specs=(whole, whole, whole, whole),
        scratch_shapes=[
            vm((4, 2, 4, 2, G, d), BF),
            vm((G, d), BF),
            vm((1, TOKENS), jnp.int32),
            vm((d, f), BF),
            vm((d, f), BF),
            vm((f, d), BF),
            vm((4, 2, 4, G, wx), BF),
            vm((4, 2, 4, G, wz), BF),
            vm((4, 2, G, cx), BF),
            vm((4, 2, G, wx - cx), BF),
            vm((4, G, cz), BF),
            vm((4, G, wz - cz), BF),
            vm((4, 2, 2, G, wx), BF),
            vm((4, 2, G, wz), BF),
            vm((4, G, wx), BF),
            vm((4, G, wx), BF),
            vm((4, 4, G, wz), BF),
            vm((4, 2, 4, G, wx), BF),
            vm((4, 2, 4, G, wz), BF),
            vm((4, 2, 4, G, d), BF),
            vm((4, 4, G, d), BF),
            vm((4, 4, G, d), BF),
            vm((4, 3, G, d), BF),
            vm((3, G, d), BF),
            vm((3, G, d), BF),
            vm((3, G, d), BF),
            vm((d, TOKENS), BF),
            vm((f, TOKENS), BF),
            vm((TOKENS, d), BF),
            dma((SENDS,)),
            dma((6,)),
            dma((4, 2, 4)),
            dma((4, 2)),
            dma((4, 2)),
            dma((4, 2, 2)),
            dma((4, 2, 2)),
            dma((4,)),
            dma((4,)),
            dma((4, 2, 4)),
            dma((4, 2, 4)),
            dma((4, 2)),
            dma((4, 2)),
            dma((4,)),
            dma((4, 3)),
            dma((3,)),
            dma((3,)),
        ],
        compiler_params=pltpu.CompilerParams(
            collective_id=0, has_side_effects=True, vmem_limit_bytes=VMEM_LIMIT
        ),
    )(tokens, grad_output, segment_ids.reshape(1, TOKENS), gate_weight, up_weight, down_weight)
    return pl.pallas_call(
        store,
        out_shape=tuple(jax.ShapeDtypeStruct(a.shape, a.dtype) for a in held),
        in_specs=[hbm] * 4,
        out_specs=(hbm,) * 4,
        scratch_shapes=[dma((4,))],
        compiler_params=pltpu.CompilerParams(vmem_limit_bytes=1 << 20),
    )(*[pltpu.with_memory_space_constraint(a, pltpu.VMEM) for a in held])


def solution(mesh):
    in_specs = (
        P("col", "row"),
        P("col", "row"),
        P("row", "col"),
        P("row", "col"),
        P("col", "row"),
        P(),
    )
    out_specs = (P("col", "row"), P("row", "col"), P("row", "col"), P("col", "row"))
    return jax.shard_map(
        per_device, mesh=mesh, in_specs=in_specs, out_specs=out_specs, check_vma=False
    )
```

```python
import functools

import jax
import jax.numpy as jnp
from jax import lax
from jax.experimental import pallas as pl
from jax.experimental.pallas import tpu as pltpu
from jax.sharding import PartitionSpec as P

MESH = pl.DeviceIdType.MESH
BF = jnp.bfloat16
F32 = jnp.float32
TOKENS = 512
SEGS = 64
G = 16
ORDER = (0, 1, 3, 2)
X_SHARE, ALL = 12, 21


def nn(a, b):
    return jnp.dot(a, b, preferred_element_type=F32)


def nt(a, b):
    return lax.dot_general(a, b, (((1,), (1,)), ((), ())), preferred_element_type=F32)


def widths(f):
    wx = 3 * f * X_SHARE // ALL
    wz = 3 * f - wx
    return wx, wz, (wx // 256) * 128, ((wz + 128) // 256) * 128


def kernel(
    tokens, grad, ids, gate_w, up_w, down_w,
    o_tok, o_gate, o_up, o_down,
    tw, gst, idv, gw, uw, dw, px, pz, rpx, rmx, rpz, rmz, lx, lz, zs, zr, zbig, hx, hz,
    gt, sib, ysend, yland, ycross, zsend, zland, tok_t, hid_t, w_st,
    ssem, loc, a_recv, rx_recv, rz_recv, lx_recv, lz_recv, zr_recv, zb_recv,
    hx_recv, hz_recv, gx_recv, gz_recv, s_recv, y_recv, yc_recv, zh_recv,
):
    d, f = gw.shape
    wx, wz, cx, cz = widths(f)
    r, c = lax.axis_index("row"), lax.axis_index("col")
    x, zl = r % 4, r // 4
    core, zh, y = c % 2, (c // 2) % 4, c // 8
    xp, xm, x2 = (x + 1) % 4, (x + 3) % 4, (x + 2) % 4

    def at(x=x, zl=zl, y=y, zh=zh, core=core):
        return {"row": zl * 4 + x, "col": (y * 4 + zh) * 2 + core}

    dev_xp, dev_xm, dev_z, dev_core = at(x=xp), at(x=xm), at(zl=1 - zl), at(core=1 - core)
    dev_zh = [at(zh=(zh + k) % 4) for k in (1, 2, 3)]
    dev_y = [at(y=(y + k) % 4) for k in (1, 2, 3)]
    dev_yc = [at(y=(y + k) % 4, core=1 - core) for k in (1, 2, 3)]
    partners = [dev_xp, dev_xm, dev_z, dev_core] + dev_zh + dev_y + dev_yc

    barrier = pltpu.get_barrier_semaphore()
    for p in partners:
        pl.semaphore_signal(barrier, inc=1, device_id=p, device_id_type=MESH)

    first = [
        pltpu.make_async_copy(tokens, tw.at[zh, core, y, 0], loc.at[0]),
        pltpu.make_async_copy(grad, gst, loc.at[1]),
        pltpu.make_async_copy(ids, idv, loc.at[5]),
    ]
    weights = [
        pltpu.make_async_copy(gate_w, gw, loc.at[2]),
        pltpu.make_async_copy(up_w, uw, loc.at[3]),
        pltpu.make_async_copy(down_w, dw, loc.at[4]),
    ]
    for cp in first + weights:
        cp.start()

    for cp in first:
        cp.wait()
    idr = jnp.broadcast_to(idv[...].astype(F32), (G, TOKENS))
    lane = lax.broadcasted_iota(jnp.int32, (G, TOKENS), 1)
    row = lax.broadcasted_iota(jnp.int32, (G, TOKENS), 0)
    mine = jnp.sum(jnp.where(lane == c * G + row, idr, 0.0), axis=1, keepdims=True)
    count = jnp.sum(jnp.where(idr == mine, 1.0, 0.0), axis=1, keepdims=True)
    weight = (TOKENS / SEGS) / count
    tw[zh, core, y, 1] = (gst[...].astype(F32) * weight).astype(BF)
    pl.semaphore_wait(barrier, len(partners))

    sent = []

    def push(src, dst, recv, dev):
        cp = pltpu.make_async_remote_copy(
            src_ref=src, dst_ref=dst, send_sem=ssem.at[len(sent)], recv_sem=recv,
            device_id=dev, device_id_type=MESH,
        )
        cp.start()
        sent.append(cp)

    def arrived(ref, recv):
        pltpu.make_async_remote_copy(
            src_ref=ref, dst_ref=ref, send_sem=ssem.at[0], recv_sem=recv,
            device_id=dev_core, device_id_type=MESH,
        ).wait_recv()

    def spread(hh, targets):
        piece = tw.at[hh, core, y]
        for dev in targets:
            push(piece, piece, a_recv.at[hh, core, y], dev)

    def gather_own():
        spread(zh, [dev_zh[0], dev_zh[2], dev_zh[1]])
        spread(zh, [dev_y[0], dev_y[2], dev_y[1], dev_core])

    def gather_far(j):
        hh = (zh + ORDER[j]) % 4
        arrived(tw.at[hh, core, y], a_recv.at[hh, core, y])
        spread(hh, [dev_y[0], dev_y[2], dev_y[1], dev_core])

    def gather_line(j):
        hh = (zh + ORDER[j]) % 4
        for k in (1, 3, 2):
            piece = tw.at[hh, core, (y + k) % 4]
            arrived(piece, a_recv.at[hh, core, (y + k) % 4])
            push(piece, piece, a_recv.at[hh, core, (y + k) % 4], dev_core)

    def multiply(j):
        hh = (zh + ORDER[j]) % 4
        for yy in range(4):
            arrived(tw.at[hh, 1 - core, yy], a_recv.at[hh, 1 - core, yy])
        t = tw[hh, :, :, 0].reshape(8 * G, d)
        w = tw[hh, :, :, 1].reshape(8 * G, d)
        if j == 0:
            for cp in weights:
                cp.wait()
        p = nn(t, uw[...]).astype(BF).reshape(2, 4, G, f)
        px[j, :, :, :, f:wx] = p[:, :, :, : wx - f]
        pz[j, :, :, :, : 2 * f - wx] = p[:, :, :, wx - f :]
        pz[j, :, :, :, 2 * f - wx :] = nt(w, dw[...]).astype(BF).reshape(2, 4, G, f)
        push(pz.at[j, 1 - zl], zbig.at[j], zb_recv.at[j], dev_z)
        px[j, :, :, :, 0:f] = nn(t, gw[...]).astype(BF).reshape(2, 4, G, f)
        relay_x(j)
        tok_t[:, j * 8 * G : (j + 1) * 8 * G] = t.T
        w_st[j * 8 * G : (j + 1) * 8 * G, :] = w

    def relay_x(j):
        push(px.at[j, :, x2, :, :cx], rpx.at[j], rx_recv.at[j, 0], dev_xp)
        push(px.at[j, :, x2, :, cx:], rmx.at[j], rx_recv.at[j, 1], dev_xm)
        push(px.at[j, :, xp, :, cx:], lx.at[j, 0, :, :, cx:], lx_recv.at[j, 0, 1], dev_xp)
        push(px.at[j, :, xm, :, :cx], lx.at[j, 1, :, :, :cx], lx_recv.at[j, 1, 0], dev_xm)

    def relay_z(j):
        push(pz.at[j, zl, x2, :, :cz], rpz.at[j], rz_recv.at[j, 0], dev_xp)
        push(pz.at[j, zl, x2, :, cz:], rmz.at[j], rz_recv.at[j, 1], dev_xm)
        push(pz.at[j, zl, xp, :, cz:], lz.at[j, 0, :, cz:], lz_recv.at[j, 0, 1], dev_xp)
        push(pz.at[j, zl, xm, :, :cz], lz.at[j, 1, :, :cz], lz_recv.at[j, 1, 0], dev_xm)

    def pair_first(j):
        arrived(zbig.at[j], zb_recv.at[j])
        pz[j, zl] = (pz[j, zl].astype(F32) + zbig[j].astype(F32)).astype(BF)
        relay_z(j)

    def forward_x(j):
        arrived(rpx.at[j], rx_recv.at[j, 0])
        rpx[j] = (px[j, :, xp, :, :cx].astype(F32) + rpx[j].astype(F32)).astype(BF)
        push(rpx.at[j], lx.at[j, 0, :, :, :cx], lx_recv.at[j, 0, 0], dev_xp)
        arrived(rmx.at[j], rx_recv.at[j, 1])
        rmx[j] = (px[j, :, xm, :, cx:].astype(F32) + rmx[j].astype(F32)).astype(BF)
        push(rmx.at[j], lx.at[j, 1, :, :, cx:], lx_recv.at[j, 1, 1], dev_xm)

    def forward_z(j):
        arrived(rpz.at[j], rz_recv.at[j, 0])
        rpz[j] = (pz[j, zl, xp, :, :cz].astype(F32) + rpz[j].astype(F32)).astype(BF)
        push(rpz.at[j], lz.at[j, 0, :, :cz], lz_recv.at[j, 0, 0], dev_xp)
        arrived(rmz.at[j], rz_recv.at[j, 1])
        rmz[j] = (pz[j, zl, xm, :, cz:].astype(F32) + rmz[j].astype(F32)).astype(BF)
        push(rmz.at[j], lz.at[j, 1, :, cz:], lz_recv.at[j, 1, 1], dev_xm)

    def sum_x(j, z):
        return px[j, z, x].astype(F32) + lx[j, 0, z].astype(F32) + lx[j, 1, z].astype(F32)

    def pair_last(j):
        for n in range(2):
            arrived(lx.at[j, n, :, :, :cx], lx_recv.at[j, n, 0])
            arrived(lx.at[j, n, :, :, cx:], lx_recv.at[j, n, 1])
        zs[j] = sum_x(j, 1 - zl).astype(BF)
        push(zs.at[j], zr.at[j], zr_recv.at[j], dev_z)

    def share_x(j, z, xx, targets):
        piece = hx.at[j, z, xx]
        for dev in targets:
            push(piece, piece, hx_recv.at[j, z, xx], dev)

    def share_z(j, xx, targets):
        piece = hz.at[j, zl, xx]
        for dev in targets:
            push(piece, piece, hz_recv.at[j, zl, xx], dev)

    def element(j):
        for n in range(2):
            arrived(lz.at[j, n, :, :cz], lz_recv.at[j, n, 0])
            arrived(lz.at[j, n, :, cz:], lz_recv.at[j, n, 1])
        arrived(zr.at[j], zr_recv.at[j])
        tx = sum_x(j, zl) + zr[j].astype(F32)
        tz = pz[j, zl, x].astype(F32) + lz[j, 0].astype(F32) + lz[j, 1].astype(F32)
        gate, dh = tx[:, :f], tz[:, 2 * f - wx :]
        up = jnp.concatenate([tx[:, f:], tz[:, : 2 * f - wx]], axis=1)
        sig = jax.nn.sigmoid(gate)
        act = gate * sig
        hx[j, zl, x, :, 0:f] = (act * up).astype(BF)
        d_gate = (dh * up * sig * (1.0 + gate * (1.0 - sig))).astype(BF)
        hx[j, zl, x, :, f:wx] = d_gate[:, : wx - f]
        hz[j, zl, x, :, : 2 * f - wx] = d_gate[:, wx - f :]
        hz[j, zl, x, :, 2 * f - wx :] = (dh * act).astype(BF)
        share_x(j, zl, x, [dev_z, dev_xp, dev_xm])
        share_z(j, x, [dev_xp, dev_xm, dev_z])

    def pair_share(j):
        arrived(hx.at[j, 1 - zl, x], hx_recv.at[j, 1 - zl, x])
        share_x(j, 1 - zl, x, [dev_xp, dev_xm])

    def line_share_x(j):
        for src, half, dev, n in ((xm, slice(0, cx), dev_xp, 0), (xp, slice(cx, wx), dev_xm, 1)):
            for z in range(2):
                arrived(hx.at[j, z, src], hx_recv.at[j, z, src])
            piece = hx.at[j, :, src, :, half]
            push(piece, piece, gx_recv.at[j, n], dev)

    def line_share_z(j):
        for src, half, dev, n in ((xm, slice(0, cz), dev_xp, 0), (xp, slice(cz, wz), dev_xm, 1)):
            arrived(hz.at[j, zl, src], hz_recv.at[j, zl, src])
            piece = hz.at[j, zl, src, :, half]
            push(piece, piece, gz_recv.at[j, n], dev)
            share_z(j, src, [dev_z])

    def far_share(j):
        arrived(hz.at[j, zl, x2, :, :cz], gz_recv.at[j, 0])
        arrived(hz.at[j, zl, x2, :, cz:], gz_recv.at[j, 1])
        share_z(j, x2, [dev_z])

    def d_gate_of(j):
        left = hx[j, :, :, :, f:wx]
        right = hz[j, :, :, :, : 2 * f - wx]
        return jnp.concatenate([left, right], axis=-1).reshape(8 * G, f)

    def d_up_of(j):
        return hz[j, :, :, :, 2 * f - wx :].reshape(8 * G, f)

    def back(j):
        arrived(hx.at[j, :, x2, :, :cx], gx_recv.at[j, 0])
        arrived(hx.at[j, :, x2, :, cx:], gx_recv.at[j, 1])
        for xx in range(4):
            arrived(hz.at[j, 1 - zl, xx], hz_recv.at[j, 1 - zl, xx])
        back_sum = nt(d_gate_of(j), gw[...]) + nt(d_up_of(j), uw[...])
        gt[j] = back_sum.astype(BF).reshape(2, 4, G, d)
        if j > 0:
            push(gt.at[j, 1 - core], sib.at[j], s_recv.at[j], dev_core)
        else:
            for k in (1, 0, 2):
                yy = (y + k + 1) % 4
                push(gt.at[j, core, yy], yland.at[j, k], y_recv.at[j, k], dev_y[k])
                push(gt.at[j, 1 - core, yy], ycross.at[k], yc_recv.at[k], dev_yc[k])
            push(gt.at[j, 1 - core, y], sib.at[j, y], s_recv.at[j], dev_core)
        hid_t[:, j * 8 * G : (j + 1) * 8 * G] = hx[j, :, :, :, 0:f].reshape(8 * G, f).T

    def core_sum(j):
        arrived(sib.at[j], s_recv.at[j])
        ysend[j] = (gt[j, core].astype(F32) + sib[j].astype(F32)).astype(BF)
        for k in (1, 0, 2):
            push(ysend.at[j, (y + k + 1) % 4], yland.at[j, k], y_recv.at[j, k], dev_y[k])

    def y_total(j):
        total = gt[j, core, y].astype(F32) + sib[j, y].astype(F32)
        for k in range(3):
            arrived(yland.at[j, k], y_recv.at[j, k])
            total = total + yland[j, k].astype(F32)
        return total

    def y_sum(j):
        zsend[j - 1] = y_total(j).astype(BF)
        push(zsend.at[j - 1], zland.at[j - 1], zh_recv.at[j - 1], dev_zh[ORDER[j] - 1])

    def finish():
        arrived(sib.at[0, y], s_recv.at[0])
        total = y_total(0)
        for k in range(3):
            arrived(ycross.at[k], yc_recv.at[k])
            total = total + ycross[k].astype(F32)
        for k in range(3):
            arrived(zland.at[k], zh_recv.at[k])
            total = total + zland[k].astype(F32)
        o_tok[...] = total.astype(BF)

    def weight_grad(lhs, rhs, out):
        rows = 256 if lhs.shape[0] % 256 == 0 else 128
        for m in range(0, lhs.shape[0], rows):
            out[m : m + rows, :] = nn(lhs[m : m + rows, :], rhs).astype(BF)

    def grad_down():
        weight_grad(hid_t, w_st[...], o_down)

    def grad_gate():
        weight_grad(tok_t, jnp.concatenate([d_gate_of(j) for j in range(4)], axis=0), o_gate)

    def grad_up():
        weight_grad(tok_t, jnp.concatenate([d_up_of(j) for j in range(4)], axis=0), o_up)

    gather_own()
    gather_far(2)
    gather_line(0)
    gather_far(1)
    multiply(0)
    gather_line(2)
    gather_far(3)
    forward_x(0)
    gather_line(1)
    multiply(2)
    pair_first(0)
    gather_line(3)
    multiply(1)
    forward_x(2)
    multiply(3)
    pair_first(2)
    forward_x(1)
    pair_last(2)
    pair_first(1)
    forward_z(2)
    forward_x(3)
    pair_last(0)
    forward_z(0)
    pair_last(1)
    forward_z(1)
    pair_first(3)
    element(2)
    pair_last(3)
    forward_z(3)
    element(1)
    pair_share(2)
    line_share_z(2)
    element(3)
    line_share_z(1)
    pair_share(1)
    line_share_x(2)
    far_share(2)
    far_share(1)
    pair_share(3)
    line_share_z(3)
    line_share_x(1)
    element(0)
    back(2)
    far_share(3)
    line_share_x(3)
    back(1)
    pair_share(0)
    line_share_z(0)
    core_sum(2)
    back(3)
    line_share_x(0)
    far_share(0)
    core_sum(1)
    core_sum(3)
    y_sum(2)
    back(0)
    y_sum(1)
    grad_down()
    y_sum(3)
    grad_gate()
    grad_up()
    finish()
    for cp in sent:
        cp.wait_send()


SENDS = 192
VMEM_LIMIT = 58 << 20


def store(a, b, c, d, a_out, b_out, c_out, d_out, sems):
    pairs = ((a, a_out), (b, b_out), (c, c_out), (d, d_out))
    copies = [pltpu.make_async_copy(src, dst, sems.at[n]) for n, (src, dst) in enumerate(pairs)]
    for cp in copies:
        cp.start()
    for cp in copies:
        cp.wait()


def per_device(tokens, grad_output, gate_weight, up_weight, down_weight, segment_ids):
    d, f = gate_weight.shape
    wx, wz, cx, cz = widths(f)
    vm, dma = pltpu.VMEM, pltpu.SemaphoreType.DMA
    whole = pl.BlockSpec(memory_space=pltpu.VMEM)
    hbm = pl.BlockSpec(memory_space=pl.ANY)
    held = pl.pallas_call(
        kernel,
        out_shape=(
            vm(tokens.shape, BF),
            vm(gate_weight.shape, BF),
            vm(up_weight.shape, BF),
            vm(down_weight.shape, BF),
        ),
        in_specs=[hbm] * 6,
        out_specs=(whole, whole, whole, whole),
        scratch_shapes=[
            vm((4, 2, 4, 2, G, d), BF),
            vm((G, d), BF),
            vm((1, TOKENS), jnp.int32),
            vm((d, f), BF),
            vm((d, f), BF),
            vm((f, d), BF),
            vm((4, 2, 4, G, wx), BF),
            vm((4, 2, 4, G, wz), BF),
            vm((4, 2, G, cx), BF),
            vm((4, 2, G, wx - cx), BF),
            vm((4, G, cz), BF),
            vm((4, G, wz - cz), BF),
            vm((4, 2, 2, G, wx), BF),
            vm((4, 2, G, wz), BF),
            vm((4, G, wx), BF),
            vm((4, G, wx), BF),
            vm((4, 4, G, wz), BF),
            vm((4, 2, 4, G, wx), BF),
            vm((4, 2, 4, G, wz), BF),
            vm((4, 2, 4, G, d), BF),
            vm((4, 4, G, d), BF),
            vm((4, 4, G, d), BF),
            vm((4, 3, G, d), BF),
            vm((3, G, d), BF),
            vm((3, G, d), BF),
            vm((3, G, d), BF),
            vm((d, TOKENS), BF),
            vm((f, TOKENS), BF),
            vm((TOKENS, d), BF),
            dma((SENDS,)),
            dma((6,)),
            dma((4, 2, 4)),
            dma((4, 2)),
            dma((4, 2)),
            dma((4, 2, 2)),
            dma((4, 2, 2)),
            dma((4,)),
            dma((4,)),
            dma((4, 2, 4)),
            dma((4, 2, 4)),
            dma((4, 2)),
            dma((4, 2)),
            dma((4,)),
            dma((4, 3)),
            dma((3,)),
            dma((3,)),
        ],
        compiler_params=pltpu.CompilerParams(
            collective_id=0, has_side_effects=True, vmem_limit_bytes=VMEM_LIMIT
        ),
    )(tokens, grad_output, segment_ids.reshape(1, TOKENS), gate_weight, up_weight, down_weight)
    return pl.pallas_call(
        store,
        out_shape=tuple(jax.ShapeDtypeStruct(a.shape, a.dtype) for a in held),
        in_specs=[hbm] * 4,
        out_specs=(hbm,) * 4,
        scratch_shapes=[dma((4,))],
        compiler_params=pltpu.CompilerParams(vmem_limit_bytes=1 << 20),
    )(*[pltpu.with_memory_space_constraint(a, pltpu.VMEM) for a in held])


def solution(mesh):
    in_specs = (
        P("col", "row"),
        P("col", "row"),
        P("row", "col"),
        P("row", "col"),
        P("col", "row"),
        P(),
    )
    out_specs = (P("col", "row"), P("row", "col"), P("row", "col"), P("col", "row"))
    return jax.shard_map(
        per_device, mesh=mesh, in_specs=in_specs, out_specs=out_specs, check_vma=False
    )
```
